32 devices in a mesh: groups: 2 (over y), leaf: 4 (over z), sub: 2 (over x), rep: 2 (over core).
Axes of the slice: x: 2, y: 2, z: 4, core: 2. Of those that a mesh axis runs over, the one named last changes fastest.
Arguments:
- vectors: bfloat16 [16, 131072], P(None, ('groups', 'leaf', 'sub', 'rep')), parts along dimension 1, may hold values from -6 to 6
- positions: float32 [3, 131072], P(None, ('groups', 'leaf', 'sub', 'rep')), parts along dimension 1, may hold values from 0 to 65, as said below
- leaf_bases: bfloat16 [512, 64, 256], P(('groups', 'leaf', 'sub', 'rep')), parts along dimension 0, may hold values from -0.375 to 0.375
- low_pairs: bfloat16 [480, 64, 128], P(('groups', 'leaf', 'sub', 'rep')), parts along dimension 0, may hold values from -0.625 to 0.625
- low_tiles: bfloat16 [960, 64, 256], P(('groups', 'leaf', 'sub', 'rep')), parts along dimension 0, may hold values from -0.375 to 0.375
- low_lists: int32 [960, 4], P(('groups', 'leaf', 'sub', 'rep')), parts along dimension 0, may hold values from -3 to 3, as said below
- top_pairs: bfloat16 [32, 2, 64, 128], P(('groups', 'leaf', 'sub', 'rep')), parts along dimension 0, may hold values from -0.625 to 0.625
- top_tiles: bfloat16 [32, 3, 64, 256], P(('groups', 'leaf', 'sub', 'rep')), parts along dimension 0, may hold values from -0.375 to 0.375
- top_lists: int32 [32, 3, 4], P(('groups', 'leaf', 'sub', 'rep')), parts along dimension 0, may hold values from -3 to 3, as said below
Outputs:
- first_product: bfloat16 [16, 131072], P(None, ('groups', 'leaf', 'sub', 'rep')), parts along dimension 1
- second_product: bfloat16 [16, 131072], P(None, ('groups', 'leaf', 'sub', 'rep')), parts along dimension 1
The draws below stay inside these ranges and needn't reach their ends.
There are 2 independent parts, one for each index of `groups`. The reference program is written for one: setup_inputs(seed, part) draws one part's arguments, and reference() takes and returns one part's arrays. A program takes and returns all parts, laid end to end along the dimension named above; each array names one. Nothing has to cross between parts.
Inputs may be any that keep to these rules, and one draw needn't show every extreme that they name: `positions`: point p lies in the box of its leaf l = p // 256: first coordinate (along the track) in [l / 4, l / 4 + 1), the other two in [0, 1). `low_lists`: a cluster whose index within its level is even lists -2, 2, 3 and 0, each once, in some order; one whose index is odd lists -3, -2, 2 and 0, each once, in some order. `top_lists`: a cluster whose index within its level is even lists -2, 2, 3 and 0, each once, in some order; one whose index is odd lists -3, -2, 2 and 0, each once, in some order.
All inputs are finite; a program needn't handle non-finite values.
Results may differ from the reference program's by a relative error of at most 0.015.
Values may be sent and summed in bfloat16 or wider, within the bound.
A program may use at most 64 MiB of HBM per device.

```python
import jax
import jax.numpy as jnp
from jax import lax

NVEC = 16
RANK = 64
LEAF_PTS = 256
ADM = 4
LEAF_DEV = 16
SHARDS = 16
LEAVES = 256
NPTS = 65536
LOCAL = 4
LOWC = 30
TOPL = 3
TOPE = 2


def parity_lists(key, parity):
    table = jnp.array([[-2, 2, 3, 0], [-3, -2, 2, 0]], dtype=jnp.int32)
    base = table[parity]
    scores = jax.random.randint(key, parity.shape + (4,), 0, 1 << 20, dtype=jnp.int32) * 4 + jnp.arange(4, dtype=jnp.int32)
    order = jnp.argsort(scores, axis=-1)
    return jnp.take_along_axis(base, order, axis=-1)


def draw_positions(key, part):
    key = jax.random.fold_in(key, 11)
    jitter = jax.random.uniform(key, (3, NPTS), jnp.float32)
    leaf_place = (jnp.arange(NPTS, dtype=jnp.int32) // LEAF_PTS).astype(jnp.float32) * 0.25
    zeros = jnp.zeros_like(leaf_place)
    return jitter + jnp.stack([leaf_place, zeros, zeros], axis=0)


def draw_low_lists(key, part):
    key = jax.random.fold_in(key, 21)
    parities = []
    for height in range(LOCAL):
        parities = parities + [index % 2 for index in range(LEAF_DEV >> height)]
    parity = jnp.tile(jnp.array(parities, dtype=jnp.int32), SHARDS)
    return parity_lists(key, parity)


def draw_top_lists(key, part):
    key = jax.random.fold_in(key, 31)
    devices = jnp.arange(SHARDS, dtype=jnp.int32)[:, None]
    levels = jnp.arange(TOPL, dtype=jnp.int32)[None, :]
    parity = jnp.right_shift(devices, levels) % 2
    return parity_lists(key, parity)


def steps_of(key, extent, cuts, low, largest):
    def one(dim, parts):
        heights = jax.random.uniform(jax.random.fold_in(jax.random.fold_in(key, 6), dim), (parts,), jnp.float32, low / len(cuts), largest / len(cuts))
        return jnp.repeat(jnp.exp(heights), extent[dim] // parts).reshape((-1,) + (1,) * (len(extent) - dim - 1))

    factor_of = one(*cuts[0])
    for cut in cuts[1:]:
        factor_of = factor_of * one(*cut)
    return factor_of


def normal_values(key, dims, scale, most, pieces=(), held_as=jnp.bfloat16):
    values = jax.random.normal(key, dims, jnp.float32) * scale
    if len(pieces) > 0:
        values = steps_of(key, dims, pieces, -0.22, 0.18) * values
    return jnp.clip(values, min=-most, max=most).astype(held_as)


def setup_inputs(seed: int = 0, part: int = 0) -> dict:
    arg_keys = jax.random.split(jax.random.key(seed), 10)
    own_keys = jax.random.split(jax.random.fold_in(arg_keys[9], part), 10)
    vectors = normal_values(own_keys[0], (NVEC, NPTS), 1.0, 6.0, ((1, 16),))
    positions = draw_positions(jax.random.fold_in(jax.random.fold_in(arg_keys[9], part), 71), part)
    leaf_bases = normal_values(own_keys[2], (LEAVES, RANK, LEAF_PTS), LEAF_PTS ** -0.5, 0.375, ((0, 16),))
    low_pairs = normal_values(own_keys[3], ((LEAF_DEV - 1) * SHARDS, RANK, 2 * RANK), (3 * RANK // 2) ** -0.5, 0.625, ((0, 16),))
    low_tiles = normal_values(own_keys[4], (LOWC * SHARDS, RANK, ADM * RANK), (ADM * RANK) ** -0.5, 0.375, ((0, 16),))
    low_lists = draw_low_lists(jax.random.fold_in(jax.random.fold_in(arg_keys[9], part), 71), part)
    top_pairs = normal_values(own_keys[6], (SHARDS, TOPE, RANK, 2 * RANK), (3 * RANK // 2) ** -0.5, 0.625, ((0, 16),))
    top_tiles = normal_values(own_keys[7], (SHARDS, TOPL, RANK, ADM * RANK), (ADM * RANK) ** -0.5, 0.375, ((0, 16),))
    top_lists = draw_top_lists(jax.random.fold_in(jax.random.fold_in(arg_keys[9], part), 71), part)
    return {"vectors": vectors, "positions": positions, "leaf_bases": leaf_bases, "low_pairs": low_pairs, "low_tiles": low_tiles, "low_lists": low_lists, "top_pairs": top_pairs, "top_tiles": top_tiles, "top_lists": top_lists}


AMPLITUDE = 0.15
SLOPE = 1.7320508075688772 / 0.3
OFFSETS = (-3, -2, 2, 3)

def kernel_block(targets, sources):
    square = jnp.zeros((targets.shape[1], sources.shape[1]), targets.dtype)
    for coord_index in range(3):
        delta = targets[coord_index][:, None] - sources[coord_index][None, :]
        square = square + delta * delta
    distance = jnp.sqrt(square)
    return AMPLITUDE * (1.0 + SLOPE * distance) * jnp.exp(-SLOPE * distance)

def near_field(ext_values, ext_coords, leaf_count, leaf_points):
    rows = 2 * leaf_points
    width = 8 * leaf_points
    row_leaf = jnp.arange(rows, dtype=jnp.int32) // leaf_points
    col_leaf = jnp.arange(width, dtype=jnp.int32) // leaf_points
    keep = jnp.abs(row_leaf[:, None] + 3 - col_leaf[None, :]) <= 3

    def one_block(block_index):
        start = block_index * rows
        targets = lax.dynamic_slice_in_dim(ext_coords, start + 3 * leaf_points, rows, 1)
        sources = lax.dynamic_slice_in_dim(ext_coords, start, width, 1)
        weights = jnp.where(keep, kernel_block(targets, sources), 0.0).astype(jnp.bfloat16)
        inputs = lax.dynamic_slice_in_dim(ext_values, start, width, 1)
        return lax.dot_general(inputs, weights, (((1,), (1,)), ((), ())), preferred_element_type=jnp.float32)
    blocks = lax.map(one_block, jnp.arange(leaf_count // 2, dtype=jnp.int32))
    return jnp.transpose(blocks, (1, 0, 2)).reshape(ext_values.shape[0], leaf_count * leaf_points)

def partner_product(tiles, lists, slices):
    picked = []
    for slot in range(lists.shape[1]):
        chosen = jnp.zeros_like(slices[OFFSETS[0]])
        for offset in OFFSETS:
            chosen = jnp.where((lists[:, slot] == offset)[:, None, None], slices[offset], chosen)
        picked.append(chosen)
    joined = jnp.stack(picked, axis=2)
    joined = joined.reshape(joined.shape[0], joined.shape[1], -1)
    return jnp.einsum('irq,ivq->ivr', tiles.astype(jnp.float32), joined.astype(jnp.float32))

def global_couple(tiles, lists, coeffs):
    amount = coeffs.shape[0]
    zeros = jnp.zeros((3,) + coeffs.shape[1:], coeffs.dtype)
    padded = jnp.concatenate([zeros, coeffs, zeros], axis=0)
    slices = {}
    for offset in OFFSETS:
        slices[offset] = padded[3 + offset:3 + offset + amount]
    return partner_product(tiles, lists, slices)

def join_children(child):
    parents = child.shape[0] // 2
    shaped = child.reshape(parents, 2, child.shape[1], child.shape[2])
    return jnp.transpose(shaped, (0, 2, 1, 3)).reshape(parents, child.shape[1], 2 * child.shape[2])

def split_children(spread):
    parents, columns, doubled = spread.shape
    shaped = spread.reshape(parents, columns, 2, doubled // 2)
    return jnp.transpose(shaped, (0, 2, 1, 3)).reshape(2 * parents, columns, doubled // 2)

def lift(pair, joined):
    return jnp.einsum('irq,ivq->ivr', pair.astype(jnp.float32), joined.astype(jnp.float32)).astype(jnp.bfloat16)

def lower(pair, field):
    return jnp.einsum('irq,ivr->ivq', pair.astype(jnp.float32), field.astype(jnp.float32)).astype(jnp.bfloat16)

def apply_once(vectors, ext_coords, leaf_bases, low_pairs, low_tiles, low_lists, top_pairs, top_tiles, top_lists):
    leaf_count = LEAF_DEV * SHARDS
    pad = jnp.zeros((NVEC, 3 * LEAF_PTS), vectors.dtype)
    near = near_field(jnp.concatenate([pad, vectors, pad], axis=1), ext_coords, leaf_count, LEAF_PTS)
    leaf_values = vectors.reshape(NVEC, leaf_count, LEAF_PTS)
    coeffs = [jnp.einsum('lrp,vlp->lvr', leaf_bases.astype(jnp.float32), leaf_values.astype(jnp.float32)).astype(jnp.bfloat16)]
    tiles_dev = low_tiles.reshape(SHARDS, LOWC, RANK, ADM * RANK)
    lists_dev = low_lists.reshape(SHARDS, LOWC, ADM)
    pairs_dev = low_pairs.reshape(SHARDS, LEAF_DEV - 1, RANK, 2 * RANK)
    amounts = [LEAF_DEV >> height for height in range(LOCAL)]
    starts = [sum(amounts[:height]) for height in range(LOCAL)]
    pair_starts = [sum(amounts[1:height + 1]) for height in range(LOCAL)]
    for height in range(LOCAL):
        parents = amounts[height] // 2
        pair = pairs_dev[:, pair_starts[height]:pair_starts[height] + parents].reshape(SHARDS * parents, RANK, 2 * RANK)
        coeffs.append(lift(pair, join_children(coeffs[height])))
    low_terms = []
    for height in range(LOCAL):
        stop = starts[height] + amounts[height]
        tiles = tiles_dev[:, starts[height]:stop].reshape(-1, RANK, ADM * RANK)
        lists = lists_dev[:, starts[height]:stop].reshape(-1, ADM)
        low_terms.append(global_couple(tiles, lists, coeffs[height]))
    top_coeffs = [coeffs[LOCAL]]
    for height in range(TOPL - 1):
        stride = 2 ** height
        top_coeffs.append(lift(top_pairs[::2 * stride, height], join_children(top_coeffs[height])))
    top_terms = []
    for height in range(TOPL):
        stride = 2 ** height
        top_terms.append(global_couple(top_tiles[::stride, height], top_lists[::stride, height], top_coeffs[height]))
    field = top_terms[TOPL - 1].astype(jnp.bfloat16)
    for height in range(TOPL - 2, -1, -1):
        stride = 2 ** height
        spread = lower(top_pairs[::2 * stride, height], field)
        field = (top_terms[height] + split_children(spread).astype(jnp.float32)).astype(jnp.bfloat16)
    for height in range(LOCAL - 1, -1, -1):
        parents = amounts[height] // 2
        pair = pairs_dev[:, pair_starts[height]:pair_starts[height] + parents].reshape(SHARDS * parents, RANK, 2 * RANK)
        spread = lower(pair, field)
        field = (low_terms[height] + split_children(spread).astype(jnp.float32)).astype(jnp.bfloat16)
    far = jnp.einsum('lrp,lvr->vlp', leaf_bases.astype(jnp.float32), field.astype(jnp.float32))
    return (near + far.reshape(NVEC, leaf_count * LEAF_PTS)).astype(jnp.bfloat16)

def reference(vectors, positions, leaf_bases, low_pairs, low_tiles, low_lists, top_pairs, top_tiles, top_lists):
    pad = jnp.zeros((3, 3 * LEAF_PTS), positions.dtype)
    ext_coords = jnp.concatenate([pad, positions, pad], axis=1)
    first_product = apply_once(vectors, ext_coords, leaf_bases, low_pairs, low_tiles, low_lists, top_pairs, top_tiles, top_lists)
    second_product = apply_once(first_product, ext_coords, leaf_bases, low_pairs, low_tiles, low_lists, top_pairs, top_tiles, top_lists)
    return (first_product, second_product)
```

```python
import functools

import jax
import jax.numpy as jnp
from jax import lax
from jax.experimental import pallas as pl
from jax.experimental.pallas import tpu as pltpu
from jax.sharding import PartitionSpec as P

AXES = ("leaf", "sub", "rep")
MESH = pl.DeviceIdType.MESH
F32 = jnp.float32
BF16 = jnp.bfloat16
I32 = jnp.int32
AMPLITUDE = 0.15
SLOPE = 1.7320508075688772 / 0.3
LOG2E = 1.4426950408889634
GAIN = SLOPE * LOG2E
LINEAR = AMPLITUDE / LOG2E
REACH = 3
HALO = 2
PAD = 3
FEATS = 32
UNROLL = 16


def repeat(count, step):
    if count <= UNROLL:
        for index in range(count):
            step(index)
    else:

        def once(index, carry):
            step(index)
            return carry

        lax.fori_loop(0, count, once, 0)


def dot(a, b):
    return lax.dot_general(a, b, (((1,), (0,)), ((), ())), preferred_element_type=F32)


def dot_t(a, b):
    return lax.dot_general(a, b, (((1,), (1,)), ((), ())), preferred_element_type=F32)


def twice(c):
    return jnp.concatenate([c, c], axis=1).astype(BF16)


def pieces(x):
    high = x.astype(BF16).astype(F32)
    rest = x - high
    mid = rest.astype(BF16).astype(F32)
    return high, mid, rest - mid


def kernel(
    sizes,
    vectors,
    positions,
    bases,
    low_pairs,
    low_tiles,
    low_lists,
    top_pairs,
    top_tiles,
    top_lists,
    first,
    second,
    weights,
    vx,
    nacc,
    feat_a,
    feat_b,
    tgt,
    src,
    pos_send,
    pos_recv,
    cx,
    c_send,
    c_recv,
    terms,
    low_exp,
    top_exp,
    own_exp,
    tiles_held,
    top_coeffs,
    upper_coeffs,
    pairs_held,
    sems,
):
    leaf_size, sub_size, rep_size = sizes
    shards = leaf_size * sub_size * rep_size
    leaves, rank, pts = bases.shape
    columns = vectors.shape[0]
    length = leaves * pts
    wing = REACH * pts
    levels = leaves.bit_length() - 1
    amounts = [leaves >> h for h in range(levels)]
    starts = [sum(amounts[:h]) for h in range(levels)]
    pair_starts = [sum(amounts[1 : h + 1]) for h in range(levels)]
    c_starts = [sum(amounts[:h]) + 2 * HALO * h for h in range(levels)]
    top_count = top_tiles.shape[1]
    top_edges = top_count - 1
    me = (lax.axis_index("leaf") * sub_size + lax.axis_index("sub")) * rep_size + lax.axis_index(
        "rep"
    )

    def place(s):
        return {
            "leaf": s // (sub_size * rep_size),
            "sub": (s // rep_size) % sub_size,
            "rep": s % rep_size,
        }

    names = iter(range(1000))

    def pair_of_sems():
        return sems.at[next(names)], sems.at[next(names)]

    def remote(source, dest, both, peer):
        return pltpu.make_async_remote_copy(
            src_ref=source,
            dst_ref=dest,
            send_sem=both[0],
            recv_sem=both[1],
            device_id=place(peer),
            device_id_type=MESH,
        )

    has_left = me > 0
    has_right = me < shards - 1

    class Exchange:
        def __init__(self, to_right, from_left, to_left, from_right):
            self.up = remote(to_right, from_left, pair_of_sems(), jnp.minimum(me + 1, shards - 1))
            self.down = remote(to_left, from_right, pair_of_sems(), jnp.maximum(me - 1, 0))

        def start(self):
            pl.when(has_right)(self.up.start)
            pl.when(has_left)(self.down.start)

        def arrive(self):
            pl.when(has_left)(self.up.wait_recv)
            pl.when(has_right)(self.down.wait_recv)

        def sent(self):
            pl.when(has_right)(self.up.wait_send)
            pl.when(has_left)(self.down.wait_send)

    barrier = pltpu.get_barrier_semaphore()

    def greet(k):
        pl.semaphore_signal(
            barrier, inc=1, device_id=place((me + k + 1) % shards), device_id_type=MESH
        )

    repeat(shards - 1, greet)

    lane = lax.broadcasted_iota(I32, (columns, 2 * rank), 1)
    is_left = lane < rank

    def expand(lists):
        block = lax.broadcasted_iota(I32, (lists.shape[0], 4 * rank), 1) // rank
        out = jnp.broadcast_to(lists[:, 3:4], block.shape)
        for k in range(3):
            out = jnp.where(block == k, jnp.broadcast_to(lists[:, k : k + 1], block.shape), out)
        return out

    low_exp[...] = expand(low_lists[...])
    wide = expand(top_lists[0])
    for t in range(top_count):
        own_exp[t] = jnp.broadcast_to(wide[t : t + 1], (8, 4 * rank))

    zeros_pad = jnp.zeros((PAD, columns, 2 * rank), BF16)
    for p in range(2):
        top_coeffs[p, 0:PAD] = zeros_pad
        top_coeffs[p, PAD + shards : PAD + shards + PAD] = zeros_pad
    for t in range(top_edges):
        count = shards >> (t + 1)
        upper_coeffs[t, 0:PAD] = zeros_pad
        upper_coeffs[t, PAD + count : PAD + count + PAD] = zeros_pad

    @pl.when(me == 0)
    def _():
        pos_recv[0] = jnp.zeros(pos_recv.shape[1:], F32)
        for p in range(2):
            vx[p, :, 0:wing] = jnp.zeros((columns, wing), BF16)
            c_recv[p, 0] = jnp.zeros(c_recv.shape[2:], BF16)

    @pl.when(me == shards - 1)
    def _():
        pos_recv[1] = jnp.zeros(pos_recv.shape[1:], F32)
        for p in range(2):
            vx[p, :, wing + length :] = jnp.zeros((columns, wing), BF16)
            c_recv[p, 1] = jnp.zeros(c_recv.shape[2:], BF16)

    pos_send[...] = jnp.zeros(pos_send.shape, F32)
    pos_send[0, 0:3, :] = positions[:, 0:wing]
    pos_send[1, 0:3, :] = positions[:, length - wing :]
    vx[0, :, wing : wing + length] = vectors[...]

    pl.semaphore_wait(barrier, shards - 1)

    pos_move = Exchange(pos_send.at[1], pos_recv.at[0], pos_send.at[0], pos_recv.at[1])
    pos_move.start()
    v_moves = [
        Exchange(
            vx.at[p, :, length : wing + length],
            vx.at[p, :, 0:wing],
            vx.at[p, :, wing : 2 * wing],
            vx.at[p, :, wing + length : 2 * wing + length],
        )
        for p in range(2)
    ]
    v_moves[0].start()

    tile_sems = [pair_of_sems() for t in range(top_count)]
    list_sems = [pair_of_sems() for t in range(top_count)]
    edge_sems = [pair_of_sems() for t in range(top_edges)]

    def send_tops():
        tiles_held[0] = top_tiles[0, 0]
        top_exp[0] = own_exp[0]
        for t in range(1, top_count):

            @pl.when(me % (1 << t) == 0)
            def _(t=t):
                tiles_held[t] = top_tiles[0, t]
                top_exp[t] = own_exp[t]

                def push(k):
                    remote(top_tiles.at[0, t], tiles_held.at[t], tile_sems[t], me + k + 1).start()
                    remote(own_exp.at[t], top_exp.at[t], list_sems[t], me + k + 1).start()

                repeat((1 << t) - 1, push)

        for t in range(top_edges):

            @pl.when(me % (2 << t) == 0)
            def _(t=t):
                slot = me // (2 << t)
                pairs_held[t, slot] = top_pairs[0, t]

                def push(k):
                    remote(
                        top_pairs.at[0, t],
                        pairs_held.at[t, slot],
                        edge_sems[t],
                        (me + k + 1) % shards,
                    ).start()

                repeat(shards - 1, push)

    def wait_bytes(ref, sem):
        pltpu.make_async_copy(ref, ref, sem).wait()

    def arrive_tops():
        for t in range(1, top_count):

            @pl.when(me % (1 << t) != 0)
            def _(t=t):
                wait_bytes(tiles_held.at[t], tile_sems[t][1])
                wait_bytes(top_exp.at[t], list_sems[t][1])

        for t in range(top_edges):
            count = shards >> (t + 1)

            @pl.when(me % (2 << t) == 0)
            def _(t=t, count=count):
                wait_bytes(pairs_held.at[t, 0 : count - 1], edge_sems[t][1])

            @pl.when(me % (2 << t) != 0)
            def _(t=t, count=count):
                wait_bytes(pairs_held.at[t, 0:count], edge_sems[t][1])

    def sent_tops():
        for t in range(1, top_count):

            @pl.when(me % (1 << t) == 0)
            def _(t=t):
                def one(k):
                    wait_bytes(tiles_held.at[t], tile_sems[t][0])
                    wait_bytes(top_exp.at[t], list_sems[t][0])

                repeat((1 << t) - 1, one)

        for t in range(top_edges):

            @pl.when(me % (2 << t) == 0)
            def _(t=t):
                def one(k):
                    wait_bytes(pairs_held.at[t, 0], edge_sems[t][0])

                repeat(shards - 1, one)

    c_moves = [
        Exchange(c_send.at[p, 1], c_recv.at[p, 0], c_send.at[p, 0], c_recv.at[p, 1])
        for p in range(2)
    ]
    root_sems = [pair_of_sems() for p in range(2)]

    def rows(h, j):
        begin = (c_starts[h] + HALO + j) * columns
        return slice(begin, begin + columns)

    def joined_of(left, right):
        return jnp.where(is_left, left.astype(F32), right.astype(F32)).astype(BF16)

    def upsweep(p):
        for leaf in range(leaves):
            begin = wing + leaf * pts
            cx[rows(0, leaf), :] = twice(dot_t(vx[p, :, begin : begin + pts], bases[leaf]))
        for h in range(levels):
            for i in range(amounts[h] // 2):
                joined = joined_of(cx[rows(h, 2 * i), :], cx[rows(h, 2 * i + 1), :])
                c = twice(dot_t(joined, low_pairs[pair_starts[h] + i]))
                if h + 1 < levels:
                    cx[rows(h + 1, i), :] = c
                else:
                    top_coeffs[p, PAD + me] = c

        def push(k):
            slot = top_coeffs.at[p, PAD + me]
            remote(slot, slot, root_sems[p], (me + k + 1) % shards).start()

        repeat(shards - 1, push)
        for h in range(levels):
            n = amounts[h]
            for j in range(HALO):
                at = slice((HALO * h + j) * columns, (HALO * h + j + 1) * columns)
                c_send[p, 0, at, :] = cx[rows(h, j), :]
                c_send[p, 1, at, :] = cx[rows(h, n - HALO + j), :]
        c_moves[p].start()

    def near(p, leaf):
        at = leaf + REACH
        total = dot(vx[p, :, at * pts : (at + REACH + 1) * pts], weights[at])
        for d in range(1, REACH + 1):
            begin = (at - d) * pts
            total = total + dot_t(
                vx[p, :, begin : begin + pts], weights[at - d, d * pts : (d + 1) * pts, :]
            )
        nacc[:, leaf * pts : (leaf + 1) * pts] = total

    def couple(row, before, after, far, far_offset, tile):
        before, after, far = (x.astype(F32) for x in (before, after, far))
        none = jnp.zeros_like(before)
        halves = []
        for half in range(2):
            listed = jnp.broadcast_to(row[:, half * 2 * rank : (half + 1) * 2 * rank], none.shape)
            value = jnp.where(listed == far_offset, far, none)
            value = jnp.where(listed == 2, after, value)
            value = jnp.where(listed == -2, before, value)
            halves.append(value.astype(BF16))
        return dot_t(jnp.concatenate(halves, axis=1), tile)

    def finish(p, out):
        c_moves[p].arrive()
        for h in range(levels):
            n = amounts[h]
            for j in range(HALO):
                at = slice((HALO * h + j) * columns, (HALO * h + j + 1) * columns)
                cx[rows(h, j - HALO), :] = c_recv[p, 0, at, :]
                cx[rows(h, n + j), :] = c_recv[p, 1, at, :]
        for h in range(levels):
            for i in range(amounts[h]):
                offset = -3 if i % 2 else 3
                index = starts[h] + i
                terms[index * columns : (index + 1) * columns, :] = couple(
                    low_exp[index : index + 1, :],
                    cx[rows(h, i - 2), :],
                    cx[rows(h, i + 2), :],
                    cx[rows(h, i + offset), :],
                    offset,
                    low_tiles[index],
                )

        if p == 0:
            arrive_tops()
        wait_bytes(top_coeffs.at[p, 0 : shards - 1], root_sems[p][1])

        def held(t):
            return top_coeffs.at[p] if t == 0 else upper_coeffs.at[t - 1]

        for t in range(top_edges):
            lower_level = held(t)
            upper_level = held(t + 1)

            def lift(i, t=t, lower_level=lower_level, upper_level=upper_level):
                joined = joined_of(lower_level[PAD + 2 * i], lower_level[PAD + 2 * i + 1])
                upper_level[PAD + i] = twice(dot_t(joined, pairs_held[t, i]))

            repeat(shards >> (t + 1), lift)

        field = None
        for t in range(top_count - 1, -1, -1):
            index = me // (1 << t)
            odd = index % 2
            offset = 3 - 6 * odd
            level = held(t)
            term = couple(
                top_exp[t, 0:1, :],
                level[PAD + index - 2],
                level[PAD + index + 2],
                level[PAD + index + offset],
                offset,
                tiles_held[t],
            )
            if field is not None:
                spread = dot(field, pairs_held[t, index // 2])
                share = jnp.where(
                    jnp.full((columns, rank), odd, I32) == 0, spread[:, :rank], spread[:, rank:]
                )
                term = term + share.astype(BF16).astype(F32)
            field = term.astype(BF16)

        fields = [field]
        for h in range(levels - 1, -1, -1):
            below = []
            for i in range(amounts[h]):
                if i % 2 == 0:
                    spread = dot(fields[i // 2], low_pairs[pair_starts[h] + i // 2])
                    spread = spread.astype(BF16).astype(F32)
                    share = spread[:, :rank]
                else:
                    share = spread[:, rank:]
                index = starts[h] + i
                below.append(
                    (terms[index * columns : (index + 1) * columns, :] + share).astype(BF16)
                )
            fields = below
        for leaf in range(leaves):
            at = slice(leaf * pts, (leaf + 1) * pts)
            value = (nacc[:, at] + dot(fields[leaf], bases[leaf])).astype(BF16)
            out[:, at] = value
            if p == 0:
                vx[1, :, wing + leaf * pts : wing + (leaf + 1) * pts] = value

    shift = jnp.where(
        lax.broadcasted_iota(I32, (3, pts), 0) == 0,
        (me * leaves).astype(F32) * 0.25,
        jnp.zeros((3, pts), F32),
    )
    feat_a[...] = jnp.zeros(feat_a.shape, F32)
    feat_b[...] = jnp.zeros(feat_b.shape, F32)
    feat_a[21:24, :] = jnp.ones((3, pts), F32)
    feat_b[18:21, :] = jnp.ones((3, pts), F32)

    def features(position, leaf):
        x = (position - shift) * GAIN
        high, mid, low = pieces(x)
        square = x * x
        norms = pieces(square[0:1] + square[1:2] + square[2:3])
        for k, part in enumerate((high, mid, high, mid, low, high)):
            feat_a[3 * k : 3 * k + 3, :] = part
        for k, part in enumerate((high, high, mid, mid, high, low)):
            feat_b[3 * k : 3 * k + 3, :] = -2.0 * part
        for k in range(3):
            feat_a[18 + k : 19 + k, :] = norms[k]
            feat_b[21 + k : 22 + k, :] = norms[k]
        at = slice(leaf * pts, (leaf + 1) * pts)
        tgt[:, at] = feat_a[...].astype(BF16)
        src[at, :] = jnp.transpose(feat_b[...]).astype(BF16)

    def evaluate(a):
        right = tgt[:, pl.ds(pl.multiple_of(a * pts, pts), pts)]
        for b in range(REACH + 1):
            left = src[pl.ds(pl.multiple_of((a + b) * pts, pts), pts), :]
            square = jnp.maximum(dot(left, right), 1e-30)
            u = square * lax.rsqrt(square)
            value = (AMPLITUDE + LINEAR * u) * jnp.exp2(-u)
            weights[a, b * pts : (b + 1) * pts, :] = value.astype(BF16)

    def evaluate_from(begin, end):
        def once(a, carry):
            evaluate(a)
            return carry

        lax.fori_loop(begin, end, once, 0)

    send_tops()
    upsweep(0)
    for leaf in range(leaves):
        features(positions[:, leaf * pts : (leaf + 1) * pts], leaf + REACH)
    evaluate_from(REACH, leaves)
    pos_move.arrive()
    for k in range(REACH):
        features(pos_recv[0, 0:3, k * pts : (k + 1) * pts], k)
        features(pos_recv[1, 0:3, k * pts : (k + 1) * pts], REACH + leaves + k)
    evaluate_from(0, REACH)
    evaluate_from(leaves, leaves + REACH)
    v_moves[0].arrive()
    for leaf in range(leaves):
        near(0, leaf)
    finish(0, first)

    v_moves[1].start()
    upsweep(1)
    for leaf in range(REACH, leaves - REACH):
        near(1, leaf)
    v_moves[1].arrive()
    for leaf in list(range(REACH)) + list(range(leaves - REACH, leaves)):
        near(1, leaf)
    finish(1, second)

    pos_move.sent()
    sent_tops()
    for p in range(2):
        v_moves[p].sent()
        c_moves[p].sent()
        wait_bytes(top_coeffs.at[p, 0 : shards - 1], root_sems[p][0])


def body(sizes, *args):
    vectors, positions, bases, low_pairs, low_tiles, low_lists, top_pairs, top_tiles, top_lists = (
        args
    )
    columns, length = vectors.shape
    leaves, rank, pts = bases.shape
    shards = sizes[0] * sizes[1] * sizes[2]
    levels = leaves.bit_length() - 1
    clusters = low_tiles.shape[0]
    top_count = top_tiles.shape[1]
    spread = leaves + 2 * REACH
    wing = REACH * pts
    vmem = pl.BlockSpec(memory_space=pltpu.VMEM)
    out = jax.ShapeDtypeStruct((columns, length), BF16)
    return pl.pallas_call(
        functools.partial(kernel, sizes),
        out_shape=(out, out),
        in_specs=[vmem] * 9,
        out_specs=(vmem, vmem),
        scratch_shapes=[
            pltpu.VMEM((leaves + REACH, (REACH + 1) * pts, pts), BF16),
            pltpu.VMEM((2, columns, spread * pts), BF16),
            pltpu.VMEM((columns, length), F32),
            pltpu.VMEM((FEATS, pts), F32),
            pltpu.VMEM((FEATS, pts), F32),
            pltpu.VMEM((FEATS, spread * pts), BF16),
            pltpu.VMEM((spread * pts, FEATS), BF16),
            pltpu.VMEM((2, 8, wing), F32),
            pltpu.VMEM((2, 8, wing), F32),
            pltpu.VMEM(((clusters + 2 * HALO * levels) * columns, 2 * rank), BF16),
            pltpu.VMEM((2, 2, HALO * levels * columns, 2 * rank), BF16),
            pltpu.VMEM((2, 2, HALO * levels * columns, 2 * rank), BF16),
            pltpu.VMEM((clusters * columns, rank), F32),
            pltpu.VMEM((clusters, 4 * rank), I32),
            pltpu.VMEM((top_count, 8, 4 * rank), I32),
            pltpu.VMEM((top_count, 8, 4 * rank), I32),
            pltpu.VMEM((top_count, rank, 4 * rank), BF16),
            pltpu.VMEM((2, shards + 2 * PAD, columns, 2 * rank), BF16),
            pltpu.VMEM(
                (top_count - 1, shards // 2 + 2 * PAD, columns, 2 * rank), BF16
            ),
            pltpu.VMEM((top_count - 1, shards // 2, rank, 2 * rank), BF16),
            pltpu.SemaphoreType.DMA((64,)),
        ],
        compiler_params=pltpu.CompilerParams(
            collective_id=0, has_side_effects=True, vmem_limit_bytes=48 * 1024 * 1024
        ),
    )(*args)


def solution(mesh):
    everywhere = ("groups",) + AXES
    placed = (
        P(None, everywhere),
        P(None, everywhere),
        P(everywhere, None, None),
        P(everywhere, None, None),
        P(everywhere, None, None),
        P(everywhere, None),
        P(everywhere, None, None, None),
        P(everywhere, None, None, None),
        P(everywhere, None, None),
    )
    sizes = tuple(mesh.shape[axis] for axis in AXES)
    return jax.shard_map(
        functools.partial(body, sizes),
        mesh=mesh,
        in_specs=placed,
        out_specs=(P(None, everywhere), P(None, everywhere)),
        check_vma=False,
    )
```

```python
import functools

import jax
import jax.numpy as jnp
from jax import lax
from jax.experimental import pallas as pl
from jax.experimental.pallas import tpu as pltpu
from jax.sharding import PartitionSpec as P

AXES = ("leaf", "sub", "rep")
MESH = pl.DeviceIdType.MESH
F32 = jnp.float32
BF16 = jnp.bfloat16
I32 = jnp.int32
AMPLITUDE = 0.15
SLOPE = 1.7320508075688772 / 0.3
LOG2E = 1.4426950408889634
GAIN = SLOPE * LOG2E
LINEAR = AMPLITUDE / LOG2E
REACH = 3
HALO = 2
PAD = 3
FEATS = 32
UNROLL = 16


def repeat(count, step):
    if count <= UNROLL:
        for index in range(count):
            step(index)
    else:

        def once(index, carry):
            step(index)
            return carry

        lax.fori_loop(0, count, once, 0)


def dot(a, b):
    return lax.dot_general(a, b, (((1,), (0,)), ((), ())), preferred_element_type=F32)


def dot_t(a, b):
    return lax.dot_general(a, b, (((1,), (1,)), ((), ())), preferred_element_type=F32)


def twice(c):
    return jnp.concatenate([c, c], axis=1).astype(BF16)


def pieces(x):
    high = x.astype(BF16).astype(F32)
    rest = x - high
    mid = rest.astype(BF16).astype(F32)
    return high, mid, rest - mid


def kernel(
    sizes,
    vectors_in,
    positions_in,
    bases_in,
    low_pairs_in,
    low_tiles_in,
    low_lists_in,
    top_pairs_in,
    top_tiles_in,
    top_lists_in,
    first,
    second,
    positions,
    bases,
    low_pairs,
    low_tiles,
    low_lists,
    lists_pad,
    top_pairs,
    top_tiles,
    top_lists,
    weights,
    vx,
    nacc,
    feat_a,
    feat_b,
    tgt,
    src,
    pos_send,
    pos_recv,
    cx,
    c_send,
    c_recv,
    terms,
    low_exp,
    top_exp,
    own_exp,
    tiles_held,
    top_coeffs,
    upper_coeffs,
    pairs_held,
    sems,
):
    leaf_size, sub_size, rep_size = sizes
    shards = leaf_size * sub_size * rep_size
    leaves, rank, pts = bases.shape
    columns = vectors_in.shape[0]
    length = leaves * pts
    wing = REACH * pts
    levels = leaves.bit_length() - 1
    amounts = [leaves >> h for h in range(levels)]
    starts = [sum(amounts[:h]) for h in range(levels)]
    pair_starts = [sum(amounts[1 : h + 1]) for h in range(levels)]
    c_starts = [sum(amounts[:h]) + 2 * HALO * h for h in range(levels)]
    top_count = top_tiles.shape[1]
    top_edges = top_count - 1
    me = (lax.axis_index("leaf") * sub_size + lax.axis_index("sub")) * rep_size + lax.axis_index(
        "rep"
    )

    def place(s):
        return {
            "leaf": s // (sub_size * rep_size),
            "sub": (s // rep_size) % sub_size,
            "rep": s % rep_size,
        }

    names = iter(range(1000))

    def pair_of_sems():
        return sems.at[next(names)], sems.at[next(names)]

    def remote(source, dest, both, peer):
        return pltpu.make_async_remote_copy(
            src_ref=source,
            dst_ref=dest,
            send_sem=both[0],
            recv_sem=both[1],
            device_id=place(peer),
            device_id_type=MESH,
        )

    def fetch(source, dest):
        copy = pltpu.make_async_copy(source, dest, sems.at[next(names)])
        copy.start()
        return copy

    fetch_vectors = fetch(vectors_in, vx.at[0, :, wing : wing + length])
    fetch_bases = fetch(bases_in, bases)
    fetch_positions = fetch(positions_in, positions)
    fetch_pairs = fetch(low_pairs_in, low_pairs)
    fetch_lists = [
        fetch(low_lists_in, low_lists),
        fetch(top_lists_in, top_lists),
    ]
    fetch_tops = [fetch(top_pairs_in, top_pairs), fetch(top_tiles_in, top_tiles)]
    fetch_tiles = fetch(low_tiles_in, low_tiles)

    has_left = me > 0
    has_right = me < shards - 1

    class Exchange:
        def __init__(self, to_right, from_left, to_left, from_right):
            self.up = remote(to_right, from_left, pair_of_sems(), jnp.minimum(me + 1, shards - 1))
            self.down = remote(to_left, from_right, pair_of_sems(), jnp.maximum(me - 1, 0))

        def start(self):
            pl.when(has_right)(self.up.start)
            pl.when(has_left)(self.down.start)

        def arrive(self):
            pl.when(has_left)(self.up.wait_recv)
            pl.when(has_right)(self.down.wait_recv)

        def sent(self):
            pl.when(has_right)(self.up.wait_send)
            pl.when(has_left)(self.down.wait_send)

    barrier = pltpu.get_barrier_semaphore()

    def greet(k):
        pl.semaphore_signal(
            barrier, inc=1, device_id=place((me + k + 1) % shards), device_id_type=MESH
        )

    repeat(shards - 1, greet)

    lane = lax.broadcasted_iota(I32, (columns, 2 * rank), 1)
    is_left = lane < rank

    def expand(lists):
        block = lax.broadcasted_iota(I32, (lists.shape[0], 4 * rank), 1) // rank
        out = jnp.broadcast_to(lists[:, 3:4], block.shape)
        for k in range(3):
            out = jnp.where(block == k, jnp.broadcast_to(lists[:, k : k + 1], block.shape), out)
        return out

    def expand_lists():
        for copy in fetch_lists:
            copy.wait()
        lists_pad[...] = jnp.zeros(lists_pad.shape, I32)
        lists_pad[0:4, 0 : low_lists.shape[1]] = low_lists[...]
        by_cluster = jnp.transpose(lists_pad[...])
        low_exp[...] = expand(by_cluster[: low_exp.shape[0], 0:4])
        for t in range(top_count):
            own_exp[t] = jnp.broadcast_to(expand(top_lists[t]), (8, 4 * rank))

    zeros_pad = jnp.zeros((PAD, columns, 2 * rank), BF16)
    for p in range(2):
        top_coeffs[p, 0:PAD] = zeros_pad
        top_coeffs[p, PAD + shards : PAD + shards + PAD] = zeros_pad
    for t in range(top_edges):
        count = shards >> (t + 1)
        upper_coeffs[t, 0:PAD] = zeros_pad
        upper_coeffs[t, PAD + count : PAD + count + PAD] = zeros_pad

    @pl.when(me == 0)
    def _():
        pos_recv[0] = jnp.zeros(pos_recv.shape[1:], F32)
        for p in range(2):
            vx[p, :, 0:wing] = jnp.zeros((columns, wing), BF16)
            c_recv[p, 0] = jnp.zeros(c_recv.shape[2:], BF16)

    @pl.when(me == shards - 1)
    def _():
        pos_recv[1] = jnp.zeros(pos_recv.shape[1:], F32)
        for p in range(2):
            vx[p, :, wing + length :] = jnp.zeros((columns, wing), BF16)
            c_recv[p, 1] = jnp.zeros(c_recv.shape[2:], BF16)

    pos_move = Exchange(pos_send.at[1], pos_recv.at[0], pos_send.at[0], pos_recv.at[1])
    v_moves = [
        Exchange(
            vx.at[p, :, length : wing + length],
            vx.at[p, :, 0:wing],
            vx.at[p, :, wing : 2 * wing],
            vx.at[p, :, wing + length : 2 * wing + length],
        )
        for p in range(2)
    ]

    tile_sems = [pair_of_sems() for t in range(top_count)]
    list_sems = [pair_of_sems() for t in range(top_count)]
    edge_sems = [pair_of_sems() for t in range(top_edges)]

    def send_tops():
        tiles_held[0] = top_tiles[0, 0]
        top_exp[0] = own_exp[0]
        for t in range(1, top_count):

            @pl.when(me % (1 << t) == 0)
            def _(t=t):
                tiles_held[t] = top_tiles[0, t]
                top_exp[t] = own_exp[t]

                def push(k):
                    remote(top_tiles.at[0, t], tiles_held.at[t], tile_sems[t], me + k + 1).start()
                    remote(own_exp.at[t], top_exp.at[t], list_sems[t], me + k + 1).start()

                repeat((1 << t) - 1, push)

        for t in range(top_edges):

            @pl.when(me % (2 << t) == 0)
            def _(t=t):
                slot = me // (2 << t)
                pairs_held[t, slot] = top_pairs[0, t]

                def push(k):
                    remote(
                        top_pairs.at[0, t],
                        pairs_held.at[t, slot],
                        edge_sems[t],
                        (me + k + 1) % shards,
                    ).start()

                repeat(shards - 1, push)

    def wait_bytes(ref, sem):
        pltpu.make_async_copy(ref, ref, sem).wait()

    def arrive_tops():
        for t in range(1, top_count):

            @pl.when(me % (1 << t) != 0)
            def _(t=t):
                wait_bytes(tiles_held.at[t], tile_sems[t][1])
                wait_bytes(top_exp.at[t], list_sems[t][1])

        for t in range(top_edges):
            count = shards >> (t + 1)

            @pl.when(me % (2 << t) == 0)
            def _(t=t, count=count):
                wait_bytes(pairs_held.at[t, 0 : count - 1], edge_sems[t][1])

            @pl.when(me % (2 << t) != 0)
            def _(t=t, count=count):
                wait_bytes(pairs_held.at[t, 0:count], edge_sems[t][1])

    def sent_tops():
        for t in range(1, top_count):

            @pl.when(me % (1 << t) == 0)
            def _(t=t):
                def one(k):
                    wait_bytes(tiles_held.at[t], tile_sems[t][0])
                    wait_bytes(top_exp.at[t], list_sems[t][0])

                repeat((1 << t) - 1, one)

        for t in range(top_edges):

            @pl.when(me % (2 << t) == 0)
            def _(t=t):
                def one(k):
                    wait_bytes(pairs_held.at[t, 0], edge_sems[t][0])

                repeat(shards - 1, one)

    c_moves = [
        Exchange(c_send.at[p, 1], c_recv.at[p, 0], c_send.at[p, 0], c_recv.at[p, 1])
        for p in range(2)
    ]
    root_sems = [pair_of_sems() for p in range(2)]

    def rows(h, j):
        begin = (c_starts[h] + HALO + j) * columns
        return slice(begin, begin + columns)

    def joined_of(left, right):
        return jnp.where(is_left, left.astype(F32), right.astype(F32)).astype(BF16)

    def upsweep(p):
        for leaf in range(leaves):
            begin = wing + leaf * pts
            cx[rows(0, leaf), :] = twice(dot_t(vx[p, :, begin : begin + pts], bases[leaf]))
        for h in range(levels):
            for i in range(amounts[h] // 2):
                joined = joined_of(cx[rows(h, 2 * i), :], cx[rows(h, 2 * i + 1), :])
                c = twice(dot_t(joined, low_pairs[pair_starts[h] + i]))
                if h + 1 < levels:
                    cx[rows(h + 1, i), :] = c
                else:
                    top_coeffs[p, PAD + me] = c

        for h in range(levels):
            n = amounts[h]
            for j in range(HALO):
                at = slice((HALO * h + j) * columns, (HALO * h + j + 1) * columns)
                c_send[p, 0, at, :] = cx[rows(h, j), :]
                c_send[p, 1, at, :] = cx[rows(h, n - HALO + j), :]

    def send_coeffs(p):
        def push(k):
            slot = top_coeffs.at[p, PAD + me]
            remote(slot, slot, root_sems[p], (me + k + 1) % shards).start()

        repeat(shards - 1, push)
        c_moves[p].start()

    def near(p, leaf):
        at = leaf + REACH
        total = dot(vx[p, :, at * pts : (at + REACH + 1) * pts], weights[at])
        for d in range(1, REACH + 1):
            begin = (at - d) * pts
            total = total + dot_t(
                vx[p, :, begin : begin + pts], weights[at - d, d * pts : (d + 1) * pts, :]
            )
        nacc[:, leaf * pts : (leaf + 1) * pts] = total

    def couple(row, before, after, far, far_offset, tile):
        before, after, far = (x.astype(F32) for x in (before, after, far))
        none = jnp.zeros_like(before)
        halves = []
        for half in range(2):
            listed = jnp.broadcast_to(row[:, half * 2 * rank : (half + 1) * 2 * rank], none.shape)
            value = jnp.where(listed == far_offset, far, none)
            value = jnp.where(listed == 2, after, value)
            value = jnp.where(listed == -2, before, value)
            halves.append(value.astype(BF16))
        return dot_t(jnp.concatenate(halves, axis=1), tile)

    def finish(p, out):
        c_moves[p].arrive()
        for h in range(levels):
            n = amounts[h]
            for j in range(HALO):
                at = slice((HALO * h + j) * columns, (HALO * h + j + 1) * columns)
                cx[rows(h, j - HALO), :] = c_recv[p, 0, at, :]
                cx[rows(h, n + j), :] = c_recv[p, 1, at, :]
        for h in range(levels):
            for i in range(amounts[h]):
                offset = -3 if i % 2 else 3
                index = starts[h] + i
                terms[index * columns : (index + 1) * columns, :] = couple(
                    low_exp[index : index + 1, :],
                    cx[rows(h, i - 2), :],
                    cx[rows(h, i + 2), :],
                    cx[rows(h, i + offset), :],
                    offset,
                    low_tiles[index],
                )

        if p == 0:
            arrive_tops()
        wait_bytes(top_coeffs.at[p, 0 : shards - 1], root_sems[p][1])

        def held(t):
            return top_coeffs.at[p] if t == 0 else upper_coeffs.at[t - 1]

        for t in range(top_edges):
            lower_level = held(t)
            upper_level = held(t + 1)

            def lift(i, t=t, lower_level=lower_level, upper_level=upper_level):
                joined = joined_of(lower_level[PAD + 2 * i], lower_level[PAD + 2 * i + 1])
                upper_level[PAD + i] = twice(dot_t(joined, pairs_held[t, i]))

            repeat(shards >> (t + 1), lift)

        field = None
        for t in range(top_count - 1, -1, -1):
            index = me // (1 << t)
            odd = index % 2
            offset = 3 - 6 * odd
            level = held(t)
            term = couple(
                top_exp[t, 0:1, :],
                level[PAD + index - 2],
                level[PAD + index + 2],
                level[PAD + index + offset],
                offset,
                tiles_held[t],
            )
            if field is not None:
                spread = dot(field, pairs_held[t, index // 2])
                share = jnp.where(
                    jnp.full((columns, rank), odd, I32) == 0, spread[:, :rank], spread[:, rank:]
                )
                term = term + share.astype(BF16).astype(F32)
            field = term.astype(BF16)

        fields = [field]
        for h in range(levels - 1, -1, -1):
            below = []
            for i in range(amounts[h]):
                if i % 2 == 0:
                    spread = dot(fields[i // 2], low_pairs[pair_starts[h] + i // 2])
                    spread = spread.astype(BF16).astype(F32)
                    share = spread[:, :rank]
                else:
                    share = spread[:, rank:]
                index = starts[h] + i
                below.append(
                    (terms[index * columns : (index + 1) * columns, :] + share).astype(BF16)
                )
            fields = below
        for leaf in range(leaves):
            at = slice(leaf * pts, (leaf + 1) * pts)
            value = (nacc[:, at] + dot(fields[leaf], bases[leaf])).astype(BF16)
            out[:, at] = value
            if p == 0:
                vx[1, :, wing + leaf * pts : wing + (leaf + 1) * pts] = value

    shift = jnp.where(
        lax.broadcasted_iota(I32, (3, pts), 0) == 0,
        (me * leaves).astype(F32) * 0.25,
        jnp.zeros((3, pts), F32),
    )
    feat_a[...] = jnp.zeros(feat_a.shape, F32)
    feat_b[...] = jnp.zeros(feat_b.shape, F32)
    feat_a[21:24, :] = jnp.ones((3, pts), F32)
    feat_b[18:21, :] = jnp.ones((3, pts), F32)

    def features(position, leaf):
        x = (position - shift) * GAIN
        high, mid, low = pieces(x)
        square = x * x
        norms = pieces(square[0:1] + square[1:2] + square[2:3])
        for k, part in enumerate((high, mid, high, mid, low, high)):
            feat_a[3 * k : 3 * k + 3, :] = part
        for k, part in enumerate((high, high, mid, mid, high, low)):
            feat_b[3 * k : 3 * k + 3, :] = -2.0 * part
        for k in range(3):
            feat_a[18 + k : 19 + k, :] = norms[k]
            feat_b[21 + k : 22 + k, :] = norms[k]
        at = slice(leaf * pts, (leaf + 1) * pts)
        tgt[:, at] = feat_a[...].astype(BF16)
        src[at, :] = jnp.transpose(feat_b[...]).astype(BF16)

    def evaluate(a):
        right = tgt[:, pl.ds(pl.multiple_of(a * pts, pts), pts)]
        for b in range(REACH + 1):
            left = src[pl.ds(pl.multiple_of((a + b) * pts, pts), pts), :]
            square = jnp.maximum(dot(left, right).astype(BF16), BF16(1e-30))
            u = square * lax.rsqrt(square)
            value = (BF16(AMPLITUDE) + BF16(LINEAR) * u) * jnp.exp2(-u)
            weights[a, b * pts : (b + 1) * pts, :] = value

    def evaluate_from(begin, end):
        def once(a, carry):
            evaluate(a)
            return carry

        lax.fori_loop(begin, end, once, 0)

    fetch_vectors.wait()
    fetch_bases.wait()
    fetch_pairs.wait()
    upsweep(0)
    fetch_positions.wait()
    pos_send[...] = jnp.zeros(pos_send.shape, F32)
    pos_send[0, 0:3, :] = positions[:, 0:wing]
    pos_send[1, 0:3, :] = positions[:, length - wing :]
    expand_lists()
    for copy in fetch_tops:
        copy.wait()

    pl.semaphore_wait(barrier, shards - 1)
    pos_move.start()
    v_moves[0].start()
    send_coeffs(0)
    send_tops()
    for leaf in range(leaves):
        features(positions[:, leaf * pts : (leaf + 1) * pts], leaf + REACH)
    evaluate_from(REACH, leaves)
    pos_move.arrive()
    for k in range(REACH):
        features(pos_recv[0, 0:3, k * pts : (k + 1) * pts], k)
        features(pos_recv[1, 0:3, k * pts : (k + 1) * pts], REACH + leaves + k)
    evaluate_from(0, REACH)
    evaluate_from(leaves, leaves + REACH)
    v_moves[0].arrive()
    for leaf in range(leaves):
        near(0, leaf)
    fetch_tiles.wait()
    finish(0, first)

    v_moves[1].start()
    upsweep(1)
    send_coeffs(1)
    for leaf in range(REACH, leaves - REACH):
        near(1, leaf)
    v_moves[1].arrive()
    for leaf in list(range(REACH)) + list(range(leaves - REACH, leaves)):
        near(1, leaf)
    finish(1, second)

    pos_move.sent()
    sent_tops()
    for p in range(2):
        v_moves[p].sent()
        c_moves[p].sent()
        wait_bytes(top_coeffs.at[p, 0 : shards - 1], root_sems[p][0])


def body(sizes, *args):
    vectors, positions, bases, low_pairs, low_tiles, low_lists, top_pairs, top_tiles, top_lists = (
        args
    )
    columns, length = vectors.shape
    leaves, rank, pts = bases.shape
    shards = sizes[0] * sizes[1] * sizes[2]
    levels = leaves.bit_length() - 1
    clusters = low_tiles.shape[0]
    top_count = top_tiles.shape[1]
    spread = leaves + 2 * REACH
    wing = REACH * pts
    low_lists = jnp.transpose(low_lists)
    top_lists = jnp.transpose(top_lists, (1, 0, 2))
    vmem = pl.BlockSpec(memory_space=pltpu.VMEM)
    hbm = pl.BlockSpec(memory_space=pltpu.HBM)
    out = jax.ShapeDtypeStruct((columns, length), BF16)
    return pl.pallas_call(
        functools.partial(kernel, sizes),
        out_shape=(out, out),
        in_specs=[hbm] * 9,
        out_specs=(vmem, vmem),
        scratch_shapes=[
            pltpu.VMEM(positions.shape, F32),
            pltpu.VMEM(bases.shape, BF16),
            pltpu.VMEM(low_pairs.shape, BF16),
            pltpu.VMEM(low_tiles.shape, BF16),
            pltpu.VMEM(low_lists.shape, I32),
            pltpu.VMEM((8, 128), I32),
            pltpu.VMEM(top_pairs.shape, BF16),
            pltpu.VMEM(top_tiles.shape, BF16),
            pltpu.VMEM(top_lists.shape, I32),
            pltpu.VMEM((leaves + REACH, (REACH + 1) * pts, pts), BF16),
            pltpu.VMEM((2, columns, spread * pts), BF16),
            pltpu.VMEM((columns, length), F32),
            pltpu.VMEM((FEATS, pts), F32),
            pltpu.VMEM((FEATS, pts), F32),
            pltpu.VMEM((FEATS, spread * pts), BF16),
            pltpu.VMEM((spread * pts, FEATS), BF16),
            pltpu.VMEM((2, 8, wing), F32),
            pltpu.VMEM((2, 8, wing), F32),
            pltpu.VMEM(((clusters + 2 * HALO * levels) * columns, 2 * rank), BF16),
            pltpu.VMEM((2, 2, HALO * levels * columns, 2 * rank), BF16),
            pltpu.VMEM((2, 2, HALO * levels * columns, 2 * rank), BF16),
            pltpu.VMEM((clusters * columns, rank), F32),
            pltpu.VMEM((clusters, 4 * rank), I32),
            pltpu.VMEM((top_count, 8, 4 * rank), I32),
            pltpu.VMEM((top_count, 8, 4 * rank), I32),
            pltpu.VMEM((top_count, rank, 4 * rank), BF16),
            pltpu.VMEM((2, shards + 2 * PAD, columns, 2 * rank), BF16),
            pltpu.VMEM(
                (top_count - 1, shards // 2 + 2 * PAD, columns, 2 * rank), BF16
            ),
            pltpu.VMEM((top_count - 1, shards // 2, rank, 2 * rank), BF16),
            pltpu.SemaphoreType.DMA((64,)),
        ],
        compiler_params=pltpu.CompilerParams(
            collective_id=0, has_side_effects=True, vmem_limit_bytes=56 * 1024 * 1024
        ),
    )(
        vectors,
        positions,
        bases,
        low_pairs,
        low_tiles,
        low_lists,
        top_pairs,
        top_tiles,
        top_lists,
    )


def solution(mesh):
    everywhere = ("groups",) + AXES
    placed = (
        P(None, everywhere),
        P(None, everywhere),
        P(everywhere, None, None),
        P(everywhere, None, None),
        P(everywhere, None, None),
        P(everywhere, None),
        P(everywhere, None, None, None),
        P(everywhere, None, None, None),
        P(everywhere, None, None),
    )
    sizes = tuple(mesh.shape[axis] for axis in AXES)
    return jax.shard_map(
        functools.partial(body, sizes),
        mesh=mesh,
        in_specs=placed,
        out_specs=(P(None, everywhere), P(None, everywhere)),
        check_vma=False,
    )
```
